256 devices in a mesh: dp: 8 (over y, core), tensor: 32 (over z, x).
Axes of the slice: x: 4, y: 4, z: 8, core: 2. Of those that a mesh axis runs over, the one named last changes fastest.
Arguments:
- hidden_act: bfloat16 [4096, 28672], P('dp', 'tensor'), may hold values from -24 to 24
- upstream: bfloat16 [4096, 4096], P(('dp', 'tensor')), may hold values from -6 to 6
- rotated_weight: bfloat16 [28672, 4096], P('tensor'), may hold values from -0.09375 to 0.09375
Outputs:
- input_grad: bfloat16 [4096, 28672], P('dp', 'tensor')
- weight_grad: bfloat16 [28672, 4096], P(('tensor', 'dp'))
The draws below stay inside these ranges and needn't reach their ends.
All inputs are finite; a program needn't handle non-finite values.
Results may differ from the reference program's by a relative error of at most 0.024.
Values may be sent and summed in bfloat16 or wider, within the bound.
A program may use at most 128 MiB of HBM per device.

```python
import math
import jax
import jax.numpy as jnp
import numpy as np
from jax import lax

D = 4096
WALSH = 1024
FF = 28672
TOK_DEV = 512
TOKENS = 4096
N_DP = 8


def draw_hidden_act(key, part):
    key = jax.random.fold_in(key, 11)
    base_key, row_key, column_key = jax.random.split(key, 3)
    row_scale = jnp.exp(jax.random.uniform(row_key, (TOKENS, 1), jnp.float32, math.log(0.02), math.log(2.0)))
    column_scale = jnp.exp(jax.random.uniform(column_key, (1, FF), jnp.float32, math.log(0.3), math.log(3.0)))
    values = jax.random.normal(base_key, (TOKENS, FF), jnp.float32) * row_scale * column_scale
    return jnp.clip(values, -24.0, 24.0).astype(jnp.bfloat16)


def shard_levels(key, extent, pieces, smallest, top_value):
    loudness = 1.0
    for position, shards_of in pieces:
        draws = jax.random.uniform(jax.random.fold_in(jax.random.fold_in(key, 6), position), (shards_of,), jnp.float32, smallest / len(pieces), top_value / len(pieces))
        loudness = loudness * jnp.repeat(jnp.exp(draws), extent[position] // shards_of).reshape((-1,) + (1,) * (len(extent) - 1 - position))
    return loudness


def centred(rng, dims, width, most, pieces=(), kind=jnp.bfloat16):
    factor_of = shard_levels(rng, dims, pieces, -0.22, 0.18) if pieces else 1.0
    entries = jax.random.normal(rng, dims, jnp.float32) * width * factor_of
    return jnp.minimum(jnp.maximum(entries, -most), most).astype(kind)


def setup_inputs(seed: int = 0) -> dict:
    streams_of = jax.random.split(jax.random.key(seed), 4)
    return {
        "hidden_act": draw_hidden_act(jax.random.fold_in(streams_of[3], 71), 0),
        "upstream": centred(streams_of[1], (TOKENS, D), 1.0, 6.0, ((0, 256),)),
        "rotated_weight": centred(streams_of[2], (FF, D), D ** -0.5, 0.09375, ((0, 32),)),
    }


MEAN_FLOOR = 0.04

def paley_table():
    modulus = 13
    residues = set((value_index * value_index % modulus for value_index in range(1, modulus)))
    conference = np.zeros((modulus + 1, modulus + 1))
    conference[0, 1:] = 1.0
    conference[1:, 0] = 1.0
    for row_index in range(modulus):
        for column_index in range(modulus):
            if row_index != column_index:
                conference[1 + row_index, 1 + column_index] = 1.0 if (column_index - row_index) % modulus in residues else -1.0
    plus_block = np.array([[1.0, 1.0], [1.0, -1.0]])
    minus_block = np.array([[1.0, -1.0], [-1.0, -1.0]])
    return np.kron(conference, plus_block) + np.kron(np.eye(modulus + 1), minus_block)

def walsh_table(length):
    index_range = jnp.arange(length, dtype=jnp.int32)
    correlation = index_range[:, None] & index_range[None, :]
    parity = jnp.zeros((length, length), jnp.int32)
    for bit_index in range(length.bit_length()):
        parity = parity + (correlation >> bit_index & 1)
    return (1 - 2 * (parity % 2)).astype(jnp.float32)

def rotate(values):
    rows_count = values.shape[0]
    split_low = 2 ** ((WALSH.bit_length() - 1) // 2)
    split_high = WALSH // split_low
    hadamard = jnp.asarray(paley_table(), jnp.float32)
    highest = lax.Precision.HIGHEST
    shaped = values.reshape(rows_count, split_high, split_low, 28)
    shaped = jnp.einsum('thla,ac->thlc', shaped, hadamard, precision=highest)
    shaped = jnp.einsum('thlc,lm->thmc', shaped, walsh_table(split_low), precision=highest)
    shaped = jnp.einsum('thmc,hk->tkmc', shaped, walsh_table(split_high), precision=highest)
    return shaped.reshape(rows_count, FF) / math.sqrt(FF)

def group_clip(rotated):
    rows_count = rotated.shape[0]
    grouped = rotated.reshape(rows_count, FF // 32, 32)
    mean_sq = lax.optimization_barrier(jnp.mean(grouped * grouped, axis=2))
    radius = jnp.sqrt(jnp.maximum(mean_sq, MEAN_FLOOR))
    spread = jnp.repeat(radius, 32, axis=1)
    squash = jnp.tanh(rotated / (2.0 * spread))
    clipped = (2.0 * spread * squash).astype(jnp.bfloat16)
    trust_gate = 1.0 - squash * squash
    return (clipped, trust_gate)

def reference(hidden_act, upstream, rotated_weight):

    def group_step(weight_total, group_index):
        hidden_rows = lax.dynamic_slice_in_dim(hidden_act, group_index * TOK_DEV, TOK_DEV, 0)
        upstream_rows = lax.dynamic_slice_in_dim(upstream, group_index * TOK_DEV, TOK_DEV, 0)
        rotated = rotate(hidden_rows.astype(jnp.float32))
        clipped, trust_gate = group_clip(rotated)
        grad_rot = jnp.dot(upstream_rows, rotated_weight.T, preferred_element_type=jnp.float32)
        input_rows = rotate(trust_gate * grad_rot).astype(jnp.bfloat16)
        partial_weight = lax.dot_general(clipped, upstream_rows, (((0,), (0,)), ((), ())), preferred_element_type=jnp.float32) / math.sqrt(TOKENS)
        rounded = lax.optimization_barrier(partial_weight.astype(jnp.bfloat16))
        return (weight_total + rounded.astype(jnp.float32), input_rows)
    initial = jnp.zeros((FF, D), jnp.float32)
    weight_total, input_rows = lax.scan(group_step, initial, jnp.arange(N_DP, dtype=jnp.int32))
    input_grad = input_rows.reshape(TOKENS, FF)
    return (input_grad, weight_total.astype(jnp.bfloat16))
```

```python
import functools
import math

import jax
import jax.numpy as jnp
import numpy as np
from jax import lax
from jax.experimental import pallas as pl
from jax.experimental.pallas import tpu as pltpu
from jax.sharding import PartitionSpec as P

FF = 28672
MEAN_FLOOR = 0.04
MESH = pl.DeviceIdType.MESH


def paley_table():
    modulus = 13
    residues = set((value_index * value_index % modulus for value_index in range(1, modulus)))
    conference = np.zeros((modulus + 1, modulus + 1))
    conference[0, 1:] = 1.0
    conference[1:, 0] = 1.0
    for row_index in range(modulus):
        for column_index in range(modulus):
            if row_index != column_index:
                conference[1 + row_index, 1 + column_index] = (
                    1.0 if (column_index - row_index) % modulus in residues else -1.0
                )
    plus_block = np.array([[1.0, 1.0], [1.0, -1.0]])
    minus_block = np.array([[1.0, -1.0], [-1.0, -1.0]])
    return np.kron(conference, plus_block) + np.kron(np.eye(modulus + 1), minus_block)


def walsh_table(length):
    index = np.arange(length)
    both = index[:, None] & index[None, :]
    parity = np.zeros((length, length), np.int64)
    for bit in range(length.bit_length()):
        parity += both >> bit & 1
    return 1.0 - 2.0 * (parity % 2)


def exchange_kernel(x_ref, o_ref, send_sem, recv_sem, own_sem):
    group = lax.axis_index("dp")
    me = lax.axis_index("tensor")
    count = 32
    barrier = pltpu.get_barrier_semaphore()

    @pl.loop(1, count)
    def _(k):
        pl.semaphore_signal(barrier, inc=1, device_id=(group, (me + k) % count), device_id_type=MESH)

    pl.semaphore_wait(barrier, count - 1)
    own = pltpu.make_async_copy(x_ref.at[me], o_ref.at[me], own_sem)
    own.start()

    def copy(k):
        other = (me + k) % count
        return pltpu.make_async_remote_copy(
            src_ref=x_ref.at[other],
            dst_ref=o_ref.at[me],
            send_sem=send_sem.at[k],
            recv_sem=recv_sem.at[k],
            device_id=(group, other),
            device_id_type=MESH,
        )

    @pl.loop(1, count)
    def _(k):
        copy(k).start()

    @pl.loop(1, count)
    def _(k):
        copy(k).wait()

    own.wait()


def exchange(blocks):
    return pl.pallas_call(
        exchange_kernel,
        out_shape=jax.ShapeDtypeStruct(blocks.shape, blocks.dtype),
        in_specs=[pl.BlockSpec(memory_space=pltpu.VMEM)],
        out_specs=pl.BlockSpec(memory_space=pltpu.VMEM),
        scratch_shapes=[
            pltpu.SemaphoreType.DMA((32,)),
            pltpu.SemaphoreType.DMA((32,)),
            pltpu.SemaphoreType.DMA,
        ],
        compiler_params=pltpu.CompilerParams(
            collective_id=0, has_side_effects=True, vmem_limit_bytes=8 << 20
        ),
    )(blocks)


def rotate_tokens(terms, table):
    local = sum(
        lax.dot_general(term, table, (((2,), (0,)), ((), ())), preferred_element_type=jnp.float32)
        for term in terms
    )
    shape = local.shape
    for bit in range(5):
        pairs = local.reshape(32 >> bit + 1, 2, 1 << bit, shape[1], shape[2])
        low, high = pairs[:, 0], pairs[:, 1]
        local = jnp.stack([low + high, low - high], axis=1).reshape(shape)
    return local / math.sqrt(FF)


def group_clip(rotated):
    grouped = rotated.reshape(rotated.shape[0], rotated.shape[1], 28, 32)
    mean_sq = jnp.mean(grouped * grouped, axis=3, keepdims=True)
    radius = jnp.sqrt(jnp.maximum(mean_sq, MEAN_FLOOR))
    spread = jnp.broadcast_to(radius, grouped.shape).reshape(rotated.shape)
    squash = jnp.tanh(rotated / (2.0 * spread))
    clipped = (2.0 * spread * squash).astype(jnp.bfloat16)
    return clipped, 1.0 - squash * squash


def on_device(hidden_act, upstream, rotated_weight):
    rows, width = hidden_act.shape
    table = jnp.asarray(np.kron(walsh_table(32), paley_table()), jnp.bfloat16)
    blocks = (32, rows // 32, width)
    tokens = exchange(hidden_act.reshape(blocks))
    rotated = rotate_tokens([tokens], table)
    clipped, trust_gate = group_clip(rotated)
    clipped = exchange(clipped).reshape(rows, width)
    upstream_all = lax.all_gather(upstream, "tensor", axis=0, tiled=True)
    grad_rot = lax.dot_general(
        upstream_all, rotated_weight, (((1,), (1,)), ((), ())), preferred_element_type=jnp.float32
    ).astype(jnp.bfloat16)
    grad_tokens = exchange(grad_rot.reshape(blocks))
    weight_sum = lax.psum_scatter(
        (
            lax.dot_general(
                clipped, upstream_all, (((0,), (0,)), ((), ())), preferred_element_type=jnp.float32
            )
            / 64.0
        ).astype(jnp.bfloat16),
        "dp",
        scatter_dimension=0,
        tiled=True,
    )
    gated = trust_gate * grad_tokens.astype(jnp.float32)
    result = rotate_tokens([gated.astype(jnp.bfloat16)], table).astype(jnp.bfloat16)
    input_grad = exchange(result).reshape(rows, width)
    return input_grad, weight_sum


def solution(mesh):
    placed = (P("dp", "tensor"), P(("dp", "tensor"), None), P("tensor", None))
    return jax.shard_map(
        on_device,
        mesh=mesh,
        in_specs=placed,
        out_specs=(P("dp", "tensor"), P(("tensor", "dp"), None)),
        check_vma=False,
    )
```

```python
import functools
import math

import jax
import jax.numpy as jnp
import numpy as np
from jax import lax
from jax.experimental import pallas as pl
from jax.experimental.pallas import tpu as pltpu
from jax.sharding import PartitionSpec as P

FF = 28672
MEAN_FLOOR = 0.04
MESH = pl.DeviceIdType.MESH


def paley_table():
    modulus = 13
    residues = set((value_index * value_index % modulus for value_index in range(1, modulus)))
    conference = np.zeros((modulus + 1, modulus + 1))
    conference[0, 1:] = 1.0
    conference[1:, 0] = 1.0
    for row_index in range(modulus):
        for column_index in range(modulus):
            if row_index != column_index:
                conference[1 + row_index, 1 + column_index] = (
                    1.0 if (column_index - row_index) % modulus in residues else -1.0
                )
    plus_block = np.array([[1.0, 1.0], [1.0, -1.0]])
    minus_block = np.array([[1.0, -1.0], [-1.0, -1.0]])
    return np.kron(conference, plus_block) + np.kron(np.eye(modulus + 1), minus_block)


def walsh_table(length):
    index = np.arange(length)
    both = index[:, None] & index[None, :]
    parity = np.zeros((length, length), np.int64)
    for bit in range(length.bit_length()):
        parity += both >> bit & 1
    return 1.0 - 2.0 * (parity % 2)


NZ, NX = 8, 4
COUNT = NZ * NX
ROWS = 16
WIDTH = 896
D = 4096
HALF = D // 2
PIECE = 112
SCALE = 1.0 / math.sqrt(FF)
TILES = WIDTH // 128
F32 = jnp.float32
BF16 = jnp.bfloat16


def butterfly(values):
    shape = values.shape
    for bit in range(5):
        pairs = values.reshape(COUNT >> bit + 1, 2, 1 << bit, shape[1], shape[2])
        low, high = pairs[:, 0], pairs[:, 1]
        values = jnp.stack([low + high, low - high], axis=1).reshape(shape)
    return values


def dot(left, right):
    return lax.dot_general(left, right, (((1,), (0,)), ((), ())), preferred_element_type=F32)


def dot_t(left, right):
    return lax.dot_general(left, right, (((1,), (1,)), ((), ())), preferred_element_type=F32)


def kernel(
    hidden, upstream, table, weight, out_ref, wout_ref,
    hs, hr, kt, uall, wv, local, gate, cs, cr, ct, gs, gr, ps, rs, part, core_in, ysend, yin,
    local_sem, own_sem, h_send, h_recv, c_send, c_recv, g_send, g_recv, r_send, r_recv,
    ag_send, ag_recv, core_send, core_recv, y_send, y_recv,
):
    group = lax.axis_index("dp")
    me = lax.axis_index("tensor")
    z, x = me // NX, me % NX
    y, c = group // 2, group % 2

    loads = [
        pltpu.make_async_copy(hidden, hs, local_sem.at[0]),
        pltpu.make_async_copy(upstream.at[:, pl.ds(0, HALF)], uall.at[0, me], local_sem.at[1]),
        pltpu.make_async_copy(upstream.at[:, pl.ds(HALF, HALF)], uall.at[1, me], local_sem.at[2]),
        pltpu.make_async_copy(hidden.at[me], hr.at[me], own_sem.at[0]),
        pltpu.make_async_copy(table, kt, local_sem.at[3]),
        pltpu.make_async_copy(weight, wv, local_sem.at[4]),
    ]
    for load in loads:
        load.start()

    barrier = pltpu.get_barrier_semaphore()

    def greet(device):
        pl.semaphore_signal(barrier, inc=1, device_id=device, device_id_type=MESH)

    @pl.loop(1, COUNT)
    def _(k):
        greet((group, (me + k) % COUNT))

    greet((2 * y + 1 - c, me))

    @pl.loop(1, 4)
    def _(k):
        greet((2 * ((y + k) % 4) + c, me))

    pl.semaphore_wait(barrier, COUNT - 1 + 1 + 3)

    def block(k, source, target, send, recv):
        other = (me + k) % COUNT
        return pltpu.make_async_remote_copy(
            src_ref=source.at[other],
            dst_ref=target.at[me],
            send_sem=send.at[k],
            recv_sem=recv.at[k],
            device_id=(group, other),
            device_id_type=MESH,
        )

    def finish(source, target, send, recv):
        @pl.loop(1, COUNT)
        def _(k):
            block(k, source, target, send, recv).wait()

    def place(dz, dx):
        return ((z + dz) % NZ) * NX + (x + dx) % NX

    def hop(half, owner, target, slot):
        return pltpu.make_async_remote_copy(
            src_ref=uall.at[half, owner],
            dst_ref=uall.at[half, owner],
            send_sem=ag_send.at[slot],
            recv_sem=ag_recv.at[half, owner],
            device_id=(group, target),
            device_id_type=MESH,
        )

    def arrived(half, owner):
        hop(half, owner, place(0, 1), 0).wait_recv()

    def sideways(dz):
        owner = place(dz, 0)
        for half in range(2):
            hop(half, owner, place(0, 1), 16 + dz * 6 + half).start()
            hop(half, owner, place(0, NX - 1), 16 + dz * 6 + 2 + half).start()

    loads[1].wait()
    loads[2].wait()
    for half in range(2):
        hop(half, me, place(1, 0), half).start()
        hop(half, me, place(NZ - 1, 0), 8 + half).start()

    loads[0].wait()

    @pl.loop(1, COUNT)
    def _(k):
        block(k, hs, hr, h_send, h_recv).start()

    sideways(0)
    for step in range(1, 5):
        for half in range(2):
            if step < 4 or half == 0:
                arrived(half, place(NZ - step, 0))
                if step < 3 or (step == 3 and half == 0):
                    hop(half, place(NZ - step, 0), place(1, 0), 2 * step + half).start()
            if step < 4 or half == 1:
                arrived(half, place(step, 0))
                if step < 3 or (step == 3 and half == 1):
                    hop(half, place(step, 0), place(NZ - 1, 0), 8 + 2 * step + half).start()
        sideways(step)
        if step < 4:
            sideways(NZ - step)

    loads[3].wait()
    loads[4].wait()
    finish(hs, hr, h_send, h_recv)

    @pl.loop(0, 2)
    def _(m):
        rows = hr[pl.ds(m * 16, 16)].reshape(256, WIDTH)
        local[pl.ds(pl.multiple_of(m * 256, 256), 256), :] = dot(rows, kt[...])

    member = (
        lax.broadcasted_iota(jnp.int32, (128, 128), 0) // 32
        == lax.broadcasted_iota(jnp.int32, (128, 128), 1) // 32
    )
    mean_table = jnp.where(member, 1.0 / 32.0, 0.0).astype(BF16)

    @pl.loop(0, TILES)
    def _(j):
        lanes = pl.ds(pl.multiple_of(j * 128, 128), 128)
        rotated = butterfly(local[:, lanes].reshape(COUNT, ROWS, 128)).reshape(COUNT * ROWS, 128)
        rotated = rotated * SCALE
        square = rotated * rotated
        high = square.astype(BF16)
        low = (square - high.astype(F32)).astype(BF16)
        mean_sq = dot(high, mean_table) + dot(low, mean_table)
        floored = jnp.maximum(mean_sq, MEAN_FLOOR)
        inverse = lax.rsqrt(floored)
        squash = jnp.tanh(rotated * (0.5 * inverse))
        clipped = (2.0 * floored * inverse * squash).astype(BF16)
        cs[:, :, lanes] = clipped.reshape(COUNT, ROWS, 128)
        gate[:, :, lanes] = (1.0 - squash * squash).reshape(COUNT, ROWS, 128)

    own_clipped = pltpu.make_async_copy(cs.at[me], cr.at[me], own_sem.at[1])
    own_clipped.start()

    @pl.loop(1, COUNT)
    def _(k):
        block(k, cs, cr, c_send, c_recv).start()

    @pl.loop(0, NZ)
    def _(i):
        odd = i % 2
        dz = odd * ((i + 1) // 2) + (1 - odd) * ((NZ - i // 2) % NZ)
        for half in range(2):
            arrived(half, place(dz, NX - 1))
        hop(0, place(dz, NX - 1), place(0, 1), 16 + dz * 6 + 4).start()
        for half in range(2):
            arrived(half, place(dz, 1))
        hop(1, place(dz, 1), place(0, NX - 1), 16 + dz * 6 + 5).start()

    @pl.loop(0, NZ)
    def _(dz):
        for half in range(2):
            arrived(half, place(dz, 2))

    loads[5].wait()

    @pl.loop(0, 2)
    def _(m):
        total = dot_t(uall[0, pl.ds(m * 16, 16)].reshape(256, HALF), wv[:, pl.ds(0, HALF)])
        total += dot_t(uall[1, pl.ds(m * 16, 16)].reshape(256, HALF), wv[:, pl.ds(HALF, HALF)])
        gs[pl.ds(m * 16, 16)] = total.astype(BF16).reshape(16, ROWS, WIDTH)

        @pl.loop(m * 16, m * 16 + 16)
        def _(i):
            @pl.when(i != me)
            def _():
                block((i + COUNT - me) % COUNT, gs, gr, g_send, g_recv).start()

    own_grad = pltpu.make_async_copy(gs.at[me], gr.at[me], own_sem.at[2])
    own_grad.start()

    own_clipped.wait()
    finish(cs, cr, c_send, c_recv)

    @pl.loop(0, TILES)
    def _(j):
        lanes = pl.ds(pl.multiple_of(j * 128, 128), 128)
        ct[lanes, :] = cr[:, :, lanes].reshape(COUNT * ROWS, 128).T

    def columns(n):
        return pl.ds(pl.multiple_of(n * 1024, 1024), 1024)

    def rows_of(owner):
        return pl.ds(pl.multiple_of(owner * PIECE, 16), PIECE)

    def to_core(n, q):
        return pltpu.make_async_remote_copy(
            src_ref=part.at[rows_of(2 * q + 1 - c), columns(n)],
            dst_ref=core_in.at[q, :, columns(n)],
            send_sem=core_send.at[n, q],
            recv_sem=core_recv.at[n, q],
            device_id=(2 * y + 1 - c, me),
            device_id_type=MESH,
        )

    def to_y(n, k):
        other = (y + k) % 4
        return pltpu.make_async_remote_copy(
            src_ref=ysend.at[other, :, columns(n)],
            dst_ref=yin.at[k - 1, :, columns(n)],
            send_sem=y_send.at[n, k],
            recv_sem=y_recv.at[n, k],
            device_id=(2 * other + c, me),
            device_id_type=MESH,
        )

    def add_core(n):
        @pl.loop(1, 4)
        def _(k):
            q = (y + k) % 4
            to_core(n, q).wait_recv()
            both = part[rows_of(2 * q + c), columns(n)].astype(F32)
            both += core_in[q, :, columns(n)].astype(F32)
            ysend[q, :, columns(n)] = both.astype(BF16)
            to_y(n, k).start()

    @pl.loop(0, 4)
    def _(n):
        for piece in range(2):
            start = pl.multiple_of((n % 2) * 1024 + piece * 512, 512)
            tokens = uall[n // 2, :, :, pl.ds(start, 512)].reshape(COUNT * ROWS, 512)
            term = dot(ct[...], tokens) * (1.0 / 64.0)
            part[:, pl.ds(pl.multiple_of(n * 1024 + piece * 512, 512), 512)] = term.astype(BF16)

        @pl.loop(0, 4)
        def _(q):
            to_core(n, q).start()

        @pl.when(n > 0)
        def _():
            add_core(n - 1)

    add_core(3)

    own_grad.wait()
    finish(gs, gr, g_send, g_recv)

    @pl.loop(0, TILES)
    def _(j):
        lanes = pl.ds(pl.multiple_of(j * 128, 128), 128)
        gated = gate[:, :, lanes] * gr[:, :, lanes].astype(F32)
        ps[:, lanes] = butterfly(gated).reshape(COUNT * ROWS, 128).astype(BF16)

    @pl.loop(0, 2)
    def _(m):
        rows = ps[pl.ds(pl.multiple_of(m * 256, 256), 256), :]
        rs[pl.ds(m * 16, 16)] = (dot(rows, kt[...]) * SCALE).astype(BF16).reshape(16, ROWS, WIDTH)

        @pl.loop(m * 16, m * 16 + 16)
        def _(i):
            @pl.when(i != me)
            def _():
                block((i + COUNT - me) % COUNT, rs, out_ref, r_send, r_recv).start()

    own_result = pltpu.make_async_copy(rs.at[me], out_ref.at[me], own_sem.at[3])
    own_result.start()

    @pl.loop(0, 4)
    def _(n):
        to_core(n, y).wait_recv()

        @pl.loop(1, 4)
        def _(k):
            to_y(n, k).wait()

        @pl.loop(0, 4)
        def _(q):
            to_core(n, q).wait_send()

        both = part[rows_of(group), columns(n)].astype(F32)
        both += core_in[y, :, columns(n)].astype(F32)
        for k in range(3):
            both += yin[k, :, columns(n)].astype(F32)
        wout_ref[:, columns(n)] = both.astype(BF16)

    def sent(slot):
        hop(0, me, place(0, 1), slot).wait_send()

    for slot in (0, 1, 2, 3, 4, 5, 6, 8, 9, 10, 11, 12, 13, 15):
        sent(slot)

    @pl.loop(16, 16 + 6 * NZ)
    def _(slot):
        sent(slot)

    own_result.wait()
    finish(rs, out_ref, r_send, r_recv)


def on_device(hidden_act, upstream, rotated_weight):
    table = jnp.asarray(np.kron(walsh_table(32), paley_table()), BF16)
    blocks = (COUNT, ROWS, WIDTH)
    sems = pltpu.SemaphoreType.DMA
    input_grad, weight_grad = pl.pallas_call(
        kernel,
        out_shape=(
            jax.ShapeDtypeStruct(blocks, BF16),
            jax.ShapeDtypeStruct((PIECE, D), BF16),
        ),
        in_specs=[pl.BlockSpec(memory_space=pl.ANY)] * 4,
        out_specs=[pl.BlockSpec(memory_space=pltpu.VMEM)] * 2,
        scratch_shapes=[
            pltpu.VMEM(blocks, BF16),
            pltpu.VMEM(blocks, BF16),
            pltpu.VMEM((WIDTH, WIDTH), BF16),
            pltpu.VMEM((2, COUNT, ROWS, HALF), BF16),
            pltpu.VMEM((WIDTH, D), BF16),
            pltpu.VMEM((COUNT * ROWS, WIDTH), F32),
            pltpu.VMEM(blocks, F32),
            pltpu.VMEM(blocks, BF16),
            pltpu.VMEM(blocks, BF16),
            pltpu.VMEM((WIDTH, COUNT * ROWS), BF16),
            pltpu.VMEM(blocks, BF16),
            pltpu.VMEM(blocks, BF16),
            pltpu.VMEM((COUNT * ROWS, WIDTH), BF16),
            pltpu.VMEM(blocks, BF16),
            pltpu.VMEM((WIDTH, D), BF16),
            pltpu.VMEM((4, PIECE, D), BF16),
            pltpu.VMEM((4, PIECE, D), BF16),
            pltpu.VMEM((3, PIECE, D), BF16),
            sems((5,)),
            sems((4,)),
            sems((COUNT,)), sems((COUNT,)), sems((COUNT,)), sems((COUNT,)),
            sems((COUNT,)), sems((COUNT,)), sems((COUNT,)), sems((COUNT,)),
            sems((64,)), sems((2, COUNT)),
            sems((4, 4)), sems((4, 4)), sems((4, 4)), sems((4, 4)),
        ],
        compiler_params=pltpu.CompilerParams(
            collective_id=0, has_side_effects=True, vmem_limit_bytes=60 << 20
        ),
    )(hidden_act.reshape(blocks), upstream, table, rotated_weight)
    return input_grad.reshape(COUNT * ROWS, WIDTH), weight_grad


def solution(mesh):
    placed = (P("dp", "tensor"), P(("dp", "tensor"), None), P("tensor", None))
    return jax.shard_map(
        on_device,
        mesh=mesh,
        in_specs=placed,
        out_specs=(P("dp", "tensor"), P(("tensor", "dp"), None)),
        check_vma=False,
    )
```

```python
import functools
import math

import jax
import jax.numpy as jnp
import numpy as np
from jax import lax
from jax.experimental import pallas as pl
from jax.experimental.pallas import tpu as pltpu
from jax.sharding import PartitionSpec as P

FF = 28672
MEAN_FLOOR = 0.04
MESH = pl.DeviceIdType.MESH


def paley_table():
    modulus = 13
    residues = set((value_index * value_index % modulus for value_index in range(1, modulus)))
    conference = np.zeros((modulus + 1, modulus + 1))
    conference[0, 1:] = 1.0
    conference[1:, 0] = 1.0
    for row_index in range(modulus):
        for column_index in range(modulus):
            if row_index != column_index:
                conference[1 + row_index, 1 + column_index] = (
                    1.0 if (column_index - row_index) % modulus in residues else -1.0
                )
    plus_block = np.array([[1.0, 1.0], [1.0, -1.0]])
    minus_block = np.array([[1.0, -1.0], [-1.0, -1.0]])
    return np.kron(conference, plus_block) + np.kron(np.eye(modulus + 1), minus_block)


def walsh_table(length):
    index = np.arange(length)
    both = index[:, None] & index[None, :]
    parity = np.zeros((length, length), np.int64)
    for bit in range(length.bit_length()):
        parity += both >> bit & 1
    return 1.0 - 2.0 * (parity % 2)


NZ, NX = 8, 4
COUNT = NZ * NX
ROWS = 16
WIDTH = 896
D = 4096
HALF = D // 2
PIECE = 112
STRIP = 512
STRIPS = D // STRIP
HALF_STRIPS = STRIPS // 2
SCALE = 1.0 / math.sqrt(FF)
TILES = WIDTH // 128
HIDDEN_PARTS = (0, 0, 0, 8, 31, 31)
EARLY = 5
GRADS = (1, 1, 1, 1)
F32 = jnp.float32
BF16 = jnp.bfloat16


def butterfly(values):
    shape = values.shape
    for bit in range(5):
        pairs = values.reshape(COUNT >> bit + 1, 2, 1 << bit, shape[1], shape[2])
        low, high = pairs[:, 0], pairs[:, 1]
        values = jnp.stack([low + high, low - high], axis=1).reshape(shape)
    return values


def dot(left, right):
    return lax.dot_general(left, right, (((1,), (0,)), ((), ())), preferred_element_type=F32)


def dot_t(left, right):
    return lax.dot_general(left, right, (((1,), (1,)), ((), ())), preferred_element_type=F32)


def kernel(
    hidden, upstream, table, weight, out_ref, wout_ref,
    hs, hr, kt, uall, wv, local, gate, cs, cr, ct, gs, gr, ps, rs, part, core_in, ysend, yin, passing, wout,
    local_sem, own_sem, h_sem, c_sem, g_sem, r_sem, hop_send, ring_recv, side_recv, pass_recv,
    core_send, core_recv, y_send, far_recv, y_recv,
):
    group = lax.axis_index("dp")
    me = lax.axis_index("tensor")
    z, x = me // NX, me % NX
    y, c = group // 2, group % 2

    loads = [
        pltpu.make_async_copy(hidden, hs, local_sem.at[0]),
        pltpu.make_async_copy(upstream.at[:, pl.ds(0, HALF)], uall.at[0, x, z], local_sem.at[1]),
        pltpu.make_async_copy(upstream.at[:, pl.ds(HALF, HALF)], uall.at[1, x, z], local_sem.at[2]),
        pltpu.make_async_copy(hidden.at[me], hr.at[me], own_sem.at[0]),
        pltpu.make_async_copy(table, kt, local_sem.at[3]),
        pltpu.make_async_copy(weight, wv, local_sem.at[4]),
    ]
    for load in loads:
        load.start()

    barrier = pltpu.get_barrier_semaphore()

    def greet(device):
        pl.semaphore_signal(barrier, inc=1, device_id=device, device_id_type=MESH)

    @pl.loop(1, COUNT)
    def _(k):
        greet((group, (me + k) % COUNT))

    greet((2 * y + 1 - c, me))

    @pl.loop(1, 4)
    def _(k):
        greet((2 * ((y + k) % 4) + c, me))

    with jax.named_scope("entry"):
        pl.semaphore_wait(barrier, COUNT - 1 + 1 + 3)

    def block(other, source, place_here, target, place_there, sem):
        return pltpu.make_async_remote_copy(
            src_ref=source.at[place_here],
            dst_ref=target.at[place_there],
            send_sem=sem.at[0],
            recv_sem=sem.at[1],
            device_id=(group, other),
            device_id_type=MESH,
        )

    def partner(k):
        j, dx = k // NX, (k + 1) % NX
        dz = (1 - j % 2) * (NZ // 2 + j // 2) + j % 2 * (NZ // 2 - (j + 1) // 2)
        return (z + dz) % NZ * NX + (x + dx) % NX

    def finish(source, target, sem):
        most = pl.ds(0, COUNT - 1)
        block((me + 1) % COUNT, source, most, target, most, sem).wait()

    def slot(t):
        return t % NX * NZ + t // NX

    def hop(half, dz, dx, to_z, to_x, recv_sem):
        owner = (half, (x + dx) % NX, (z + dz) % NZ)
        return pltpu.make_async_remote_copy(
            src_ref=uall.at[owner],
            dst_ref=uall.at[owner],
            send_sem=hop_send,
            recv_sem=recv_sem,
            device_id=(group, (z + to_z) % NZ * NX + (x + to_x) % NX),
            device_id_type=MESH,
        )

    def both_arrived(recv_sem):
        pltpu.make_async_copy(uall.at[:, 0, 0], uall.at[:, 0, 0], recv_sem).wait()

    def sideways(dz):
        for half in range(2):
            hop(half, dz, 0, 0, 1, side_recv.at[0, dz]).start()
            hop(half, dz, 0, 0, NX - 1, side_recv.at[1, dz]).start()

    def send_hidden(part_index):
        @pl.loop(HIDDEN_PARTS[part_index], HIDDEN_PARTS[part_index + 1])
        def _(k):
            other = partner(k)
            block(other, hs, other, hr, me, h_sem).start()

    with jax.named_scope("ring_along_z"):
        loads[1].wait()
        loads[2].wait()
        for half in range(2):
            hop(half, 0, 0, 1, 0, ring_recv.at[0, 0]).start()
            hop(half, 0, 0, NZ - 1, 0, ring_recv.at[1, 0]).start()
        sideways(0)
        loads[0].wait()
        send_hidden(0)
        for step in range(1, 4):
            both_arrived(ring_recv.at[0, step - 1])
            for half in range(2 if step < 3 else 1):
                hop(half, NZ - step, 0, 1, 0, ring_recv.at[0, step]).start()
            both_arrived(ring_recv.at[1, step - 1])
            for half in range(0 if step < 3 else 1, 2):
                hop(half, step, 0, NZ - 1, 0, ring_recv.at[1, step]).start()
            sideways(step)
            sideways(NZ - step)
            send_hidden(step)
        hop(0, 4, 0, 1, 0, ring_recv.at[0, 3]).wait_recv()
        hop(1, 4, 0, NZ - 1, 0, ring_recv.at[1, 3]).wait_recv()
        sideways(4)
        send_hidden(4)

    def grad_group(dx):
        column = (x + dx) % NX
        total = dot_t(uall[0, column].reshape(NZ * ROWS, HALF), wv[:, pl.ds(0, HALF)])
        total += dot_t(uall[1, column].reshape(NZ * ROWS, HALF), wv[:, pl.ds(HALF, HALF)])
        gs[pl.ds(column * NZ, NZ)] = total.astype(BF16).reshape(NZ, ROWS, WIDTH)

    def send_grad(dx):
        column = (x + dx) % NX

        @pl.loop(0 if dx else 1, NZ)
        def _(dz):
            row = (z + dz) % NZ
            block(row * NX + column, gs, column * NZ + row, gr, me, g_sem).start()

    with jax.named_scope("first_grad"):
        loads[5].wait()
        grad_group(0)
        own_grad = pltpu.make_async_copy(gs.at[slot(me)], gr.at[me], own_sem.at[2])
        own_grad.start()

    def forward(i):
        odd = i % 2
        dz = odd * ((i + 1) // 2) + (1 - odd) * ((NZ - i // 2) % NZ)
        both_arrived(side_recv.at[0, dz])
        hop(0, dz, NX - 1, 0, 1, pass_recv).start()
        both_arrived(side_recv.at[1, dz])
        hop(1, dz, 1, 0, NX - 1, pass_recv).start()

    with jax.named_scope("forward_along_x"):
        pl.loop(0, EARLY)(forward)

    loads[3].wait()
    loads[4].wait()
    with jax.named_scope("wait_hidden"):
        finish(hs, hr, h_sem)

    if GRADS[0] == 0:
        send_grad(0)

    with jax.named_scope("rotate_hidden"):
        @pl.loop(0, 2)
        def _(m):
            rows = hr[pl.ds(m * 16, 16)].reshape(256, WIDTH)
            local[pl.ds(pl.multiple_of(m * 256, 256), 256), :] = dot(rows, kt[...])

    member = (
        lax.broadcasted_iota(jnp.int32, (128, 128), 0) // 32
        == lax.broadcasted_iota(jnp.int32, (128, 128), 1) // 32
    )
    mean_table = jnp.where(member, 1.0 / 32.0, 0.0).astype(BF16)

    with jax.named_scope("clip"):
        @pl.loop(0, TILES)
        def _(j):
            lanes = pl.ds(pl.multiple_of(j * 128, 128), 128)
            rotated = butterfly(local[:, lanes].reshape(COUNT, ROWS, 128)).reshape(COUNT * ROWS, 128)
            rotated = rotated * SCALE
            square = rotated * rotated
            high = square.astype(BF16)
            low = (square - high.astype(F32)).astype(BF16)
            mean_sq = dot(high, mean_table) + dot(low, mean_table)
            floored = jnp.maximum(mean_sq, MEAN_FLOOR)
            inverse = lax.rsqrt(floored)
            squash = jnp.tanh(rotated * (0.5 * inverse))
            clipped = (2.0 * floored * inverse * squash).astype(BF16)
            cs[:, :, lanes] = clipped.reshape(COUNT, ROWS, 128)
            gate[:, :, lanes] = (1.0 - squash * squash).reshape(COUNT, ROWS, 128)

    with jax.named_scope("send_clipped"):
        @pl.loop(0, COUNT - 1)
        def _(k):
            other = partner(k)
            block(other, cs, other, cr, slot(me), c_sem).start()

        own_clipped = pltpu.make_async_copy(cs.at[me], cr.at[slot(me)], own_sem.at[1])
        own_clipped.start()

    with jax.named_scope("rest_along_x"):
        pl.loop(EARLY, NZ)(forward)
    with jax.named_scope("near_grad"):
        if GRADS[0] == 1:
            send_grad(0)
        for dx in (1, NX - 1):
            grad_group(dx)
            if GRADS[dx] == 1:
                send_grad(dx)
    with jax.named_scope("wait_gather"):
        pltpu.make_async_copy(uall.at[:, 0], uall.at[:, 0], pass_recv).wait()
    with jax.named_scope("last_grad"):
        grad_group(2)
        if GRADS[2] == 1:
            send_grad(2)

    own_clipped.wait()
    with jax.named_scope("wait_clipped"):
        finish(cs, cr, c_sem)
    for dx in range(NX):
        if GRADS[dx] == 2:
            send_grad(dx)

    @pl.loop(0, TILES)
    def _(j):
        lanes = pl.ds(pl.multiple_of(j * 128, 128), 128)
        ct[lanes, :] = cr[:, :, lanes].reshape(COUNT * ROWS, 128).T

    def columns(n):
        return pl.ds(pl.multiple_of(n * STRIP, STRIP), STRIP)

    def rows_of(owner):
        return pl.ds(pl.multiple_of(owner * PIECE, 16), PIECE)

    def to_core(n, q):
        return pltpu.make_async_remote_copy(
            src_ref=part.at[rows_of(2 * q + 1 - c), columns(n)],
            dst_ref=core_in.at[q, :, columns(n)],
            send_sem=core_send,
            recv_sem=core_recv.at[n],
            device_id=(2 * y + 1 - c, me),
            device_id_type=MESH,
        )

    def to_y(n, owner, target, landing, recv_sem):
        return pltpu.make_async_remote_copy(
            src_ref=ysend.at[owner, :, columns(n)],
            dst_ref=landing,
            send_sem=y_send,
            recv_sem=recv_sem,
            device_id=(2 * target + c, me),
            device_id_type=MESH,
        )

    def far(n):
        way = 1 + 2 * (n // HALF_STRIPS)
        return to_y(n, (y + 2) % 4, (y + way) % 4, passing.at[:, columns(n)], far_recv.at[n])

    def direct(n):
        back = (y + 3 - 2 * (n // HALF_STRIPS)) % 4
        return to_y(n, back, back, yin.at[0, :, columns(n)], y_recv)

    def joined(n):
        ahead = (y + 1 + 2 * (n // HALF_STRIPS)) % 4
        return to_y(n, ahead, ahead, yin.at[1, :, columns(n)], y_recv)

    def pair(n, q):
        both = part[rows_of(2 * q + c), columns(n)].astype(F32)
        return both + core_in[q, :, columns(n)].astype(F32)

    def send_far(n):
        pltpu.make_async_copy(core_in.at[:, :, columns(n)], core_in.at[:, :, columns(n)], core_recv.at[n]).wait()
        q = (y + 2) % 4
        ysend[q, :, columns(n)] = pair(n, q).astype(BF16)
        far(n).start()

    def send_direct(n):
        q = (y + 3 - 2 * (n // HALF_STRIPS)) % 4
        ysend[q, :, columns(n)] = pair(n, q).astype(BF16)
        direct(n).start()

    def join(n):
        q = (y + 1 + 2 * (n // HALF_STRIPS)) % 4
        far(n).wait_recv()
        both = pair(n, q) + passing[:, columns(n)].astype(F32)
        ysend[q, :, columns(n)] = both.astype(BF16)
        joined(n).start()

    def turn(i):
        return (i % 2) * HALF_STRIPS + i // 2

    with jax.named_scope("weight_term"):
        @pl.loop(0, STRIPS)
        def _(i):
            n = turn(i)
            start = pl.multiple_of(n % HALF_STRIPS * STRIP, STRIP)
            tokens = uall[n // HALF_STRIPS, :, :, :, pl.ds(start, STRIP)].reshape(COUNT * ROWS, STRIP)
            term = dot(ct[...], tokens) * (1.0 / 64.0)
            part[:, columns(n)] = term.astype(BF16)

            @pl.loop(0, 4)
            def _(k):
                to_core(n, (y + 2 + k) % 4).start()

            @pl.when(i > 0)
            def _():
                send_far(turn(i - 1))

        send_far(turn(STRIPS - 1))

    with jax.named_scope("direct_along_y"):
        @pl.loop(0, STRIPS)
        def _(i):
            send_direct(turn(i))

    own_grad.wait()
    with jax.named_scope("wait_grad"):
        finish(gs, gr, g_sem)

    with jax.named_scope("rotate_grad"):
        @pl.loop(0, TILES)
        def _(j):
            lanes = pl.ds(pl.multiple_of(j * 128, 128), 128)
            gated = gate[:, :, lanes] * gr[:, :, lanes].astype(F32)
            ps[:, lanes] = butterfly(gated).reshape(COUNT * ROWS, 128).astype(BF16)

        @pl.loop(0, 2)
        def _(m):
            rows = ps[pl.ds(pl.multiple_of(m * 256, 256), 256), :]
            rs[pl.ds(m * 16, 16)] = (dot(rows, kt[...]) * SCALE).astype(BF16).reshape(16, ROWS, WIDTH)

            @pl.loop(m * 16, m * 16 + 16)
            def _(i):
                @pl.when(i != me)
                def _():
                    block(i, rs, i, out_ref, me, r_sem).start()

        own_result = pltpu.make_async_copy(rs.at[me], out_ref.at[me], own_sem.at[3])
        own_result.start()

    with jax.named_scope("join_along_y"):
        @pl.loop(0, STRIPS)
        def _(i):
            join(turn(i))

    with jax.named_scope("wait_along_y"):
        pltpu.make_async_copy(yin, yin, y_recv).wait()

    with jax.named_scope("last_sum"):
        @pl.loop(0, STRIPS)
        def _(n):
            both = pair(n, y)
            for lane in range(2):
                both += yin[lane, :, columns(n)].astype(F32)
            wout[:, columns(n)] = both.astype(BF16)

    out_copy = pltpu.make_async_copy(wout, wout_ref, own_sem.at[4])
    out_copy.start()

    pltpu.make_async_copy(core_in, core_in, core_send).wait()
    pltpu.make_async_copy(ysend.at[pl.ds(0, 3)], ysend.at[pl.ds(0, 3)], y_send).wait()
    sent = uall.at[:, :, pl.ds(0, NZ - 1)]
    pltpu.make_async_copy(sent, sent, hop_send).wait()
    sent = uall.at[:, pl.ds(0, 3), 0]
    pltpu.make_async_copy(sent, sent, hop_send).wait()
    own_result.wait()
    with jax.named_scope("wait_result"):
        finish(rs, out_ref, r_sem)
    out_copy.wait()


def settle(input_grad, weight_grad, input_out, weight_out, input_held, weight_held, sem):
    def steps(source, held, target, lane):
        cuts = [pl.ds(0, 16), pl.ds(16, source.shape[0] - 16)]
        first = [pltpu.make_async_copy(source.at[c], held.at[c], sem.at[lane, i]) for i, c in enumerate(cuts)]
        second = [pltpu.make_async_copy(held.at[c], target.at[c], sem.at[lane, i + 2]) for i, c in enumerate(cuts)]
        return list(zip(first, second))

    every = steps(input_grad, input_held, input_out, 0) + steps(weight_grad, weight_held, weight_out, 1)
    for first, second in every:
        first.start()
    for first, second in every:
        first.wait()
        second.start()
    for first, second in every:
        second.wait()


def on_device(hidden_act, upstream, rotated_weight):
    table = jnp.asarray(np.kron(walsh_table(32), paley_table()), BF16)
    blocks = (COUNT, ROWS, WIDTH)
    sems = pltpu.SemaphoreType.DMA
    input_grad, weight_grad = pl.pallas_call(
        kernel,
        out_shape=(
            jax.ShapeDtypeStruct(blocks, BF16),
            jax.ShapeDtypeStruct((PIECE, D), BF16),
        ),
        in_specs=[pl.BlockSpec(memory_space=pl.ANY)] * 4,
        out_specs=[pl.BlockSpec(memory_space=pl.ANY)] * 2,
        scratch_shapes=[
            pltpu.VMEM(blocks, BF16),
            pltpu.VMEM(blocks, BF16),
            pltpu.VMEM((WIDTH, WIDTH), BF16),
            pltpu.VMEM((2, NX, NZ, ROWS, HALF), BF16),
            pltpu.VMEM((WIDTH, D), BF16),
            pltpu.VMEM((COUNT * ROWS, WIDTH), F32),
            pltpu.VMEM(blocks, F32),
            pltpu.VMEM(blocks, BF16),
            pltpu.VMEM(blocks, BF16),
            pltpu.VMEM((WIDTH, COUNT * ROWS), BF16),
            pltpu.VMEM(blocks, BF16),
            pltpu.VMEM(blocks, BF16),
            pltpu.VMEM((COUNT * ROWS, WIDTH), BF16),
            pltpu.VMEM(blocks, BF16),
            pltpu.VMEM((WIDTH, D), BF16),
            pltpu.VMEM((4, PIECE, D), BF16),
            pltpu.VMEM((4, PIECE, D), BF16),
            pltpu.VMEM((2, PIECE, D), BF16),
            pltpu.VMEM((PIECE, D), BF16),
            pltpu.VMEM((PIECE, D), BF16),
            sems((5,)),
            sems((5,)),
            sems((2,)), sems((2,)), sems((2,)), sems((2,)),
            sems, sems((2, 4)), sems((2, NZ)), sems,
            sems, sems((STRIPS,)), sems, sems((STRIPS,)), sems,
        ],
        compiler_params=pltpu.CompilerParams(
            collective_id=0, has_side_effects=True, vmem_limit_bytes=60 << 20
        ),
    )(hidden_act.reshape(blocks), upstream, table, rotated_weight)
    input_grad, weight_grad = pl.pallas_call(
        settle,
        out_shape=(
            jax.ShapeDtypeStruct(blocks, BF16),
            jax.ShapeDtypeStruct((PIECE, D), BF16),
        ),
        in_specs=[pl.BlockSpec(memory_space=pl.ANY)] * 2,
        out_specs=[pl.BlockSpec(memory_space=pl.ANY)] * 2,
        scratch_shapes=[pltpu.VMEM(blocks, BF16), pltpu.VMEM((PIECE, D), BF16), sems((2, 4))],
    )(input_grad, weight_grad)
    return input_grad.reshape(COUNT * ROWS, WIDTH), weight_grad


def solution(mesh):
    placed = (P("dp", "tensor"), P(("dp", "tensor"), None), P("tensor", None))
    return jax.shard_map(
        on_device,
        mesh=mesh,
        in_specs=placed,
        out_specs=(P("dp", "tensor"), P(("tensor", "dp"), None)),
        check_vma=False,
    )
```

```python
import functools
import math

import jax
import jax.numpy as jnp
import numpy as np
from jax import lax
from jax.experimental import pallas as pl
from jax.experimental.pallas import tpu as pltpu
from jax.sharding import PartitionSpec as P

FF = 28672
MEAN_FLOOR = 0.04
MESH = pl.DeviceIdType.MESH


def paley_table():
    modulus = 13
    residues = set((value_index * value_index % modulus for value_index in range(1, modulus)))
    conference = np.zeros((modulus + 1, modulus + 1))
    conference[0, 1:] = 1.0
    conference[1:, 0] = 1.0
    for row_index in range(modulus):
        for column_index in range(modulus):
            if row_index != column_index:
                conference[1 + row_index, 1 + column_index] = (
                    1.0 if (column_index - row_index) % modulus in residues else -1.0
                )
    plus_block = np.array([[1.0, 1.0], [1.0, -1.0]])
    minus_block = np.array([[1.0, -1.0], [-1.0, -1.0]])
    return np.kron(conference, plus_block) + np.kron(np.eye(modulus + 1), minus_block)


def walsh_table(length):
    index = np.arange(length)
    both = index[:, None] & index[None, :]
    parity = np.zeros((length, length), np.int64)
    for bit in range(length.bit_length()):
        parity += both >> bit & 1
    return 1.0 - 2.0 * (parity % 2)


NZ, NX = 8, 4
COUNT = NZ * NX
ROWS = 16
WIDTH = 896
D = 4096
HALF = D // 2
PIECE = 112
STRIP = 512
STRIPS = D // STRIP
HALF_STRIPS = STRIPS // 2
SCALE = 1.0 / math.sqrt(FF)
TILES = WIDTH // 128
PARTS_0 = (0, 0, 0, 8, 31, 31)
PARTS_1 = (0, 0, 8, 20, 31, 31)
FORWARDS = ((), (), (), (0, 1, 7, 2, 6), (), (3, 5, 4))
LAST_AFTER = False
GRADS = ((1, 1, 1, 1), (1, 3, 3, 3))
F32 = jnp.float32
BF16 = jnp.bfloat16


def butterfly(values):
    shape = values.shape
    for bit in range(5):
        pairs = values.reshape(COUNT >> bit + 1, 2, 1 << bit, shape[1], shape[2])
        low, high = pairs[:, 0], pairs[:, 1]
        values = jnp.stack([low + high, low - high], axis=1).reshape(shape)
    return values


def dot(left, right):
    return lax.dot_general(left, right, (((1,), (0,)), ((), ())), preferred_element_type=F32)


def dot_t(left, right):
    return lax.dot_general(left, right, (((1,), (1,)), ((), ())), preferred_element_type=F32)


def kernel(
    hidden, upstream, table, weight, out_ref, wout_ref,
    hs, hr, kt, uall, wv, local, gate, cs, cr, ct, gs, gr, ps, rs, part, core_in, ysend, yin, passing, wout,
    local_sem, own_sem, h_sem, c_sem, g_sem, r_sem, hop_send, ring_recv, side_recv, pass_recv,
    core_send, core_recv, y_send, far_recv, y_recv,
):
    group = lax.axis_index("dp")
    me = lax.axis_index("tensor")
    z, x = me // NX, me % NX
    y, c = group // 2, group % 2

    loads = [
        pltpu.make_async_copy(hidden, hs, local_sem.at[0]),
        pltpu.make_async_copy(upstream.at[:, pl.ds(0, HALF)], uall.at[0, x, z], local_sem.at[1]),
        pltpu.make_async_copy(upstream.at[:, pl.ds(HALF, HALF)], uall.at[1, x, z], local_sem.at[2]),
        pltpu.make_async_copy(hidden.at[me], hr.at[me], own_sem.at[0]),
        pltpu.make_async_copy(table, kt, local_sem.at[3]),
        pltpu.make_async_copy(weight, wv, local_sem.at[4]),
    ]
    for load in loads:
        load.start()

    barrier = pltpu.get_barrier_semaphore()

    def greet(device):
        pl.semaphore_signal(barrier, inc=1, device_id=device, device_id_type=MESH)

    @pl.loop(1, COUNT)
    def _(k):
        greet((group, (me + k) % COUNT))

    greet((2 * y + 1 - c, me))

    @pl.loop(1, 4)
    def _(k):
        greet((2 * ((y + k) % 4) + c, me))

    with jax.named_scope("entry"):
        pl.semaphore_wait(barrier, COUNT - 1 + 1 + 3)

    def block(other, source, place_here, target, place_there, sem):
        return pltpu.make_async_remote_copy(
            src_ref=source.at[place_here],
            dst_ref=target.at[place_there],
            send_sem=sem.at[0],
            recv_sem=sem.at[1],
            device_id=(group, other),
            device_id_type=MESH,
        )

    def partner(k):
        j, dx = k // NX, (k + 1) % NX
        dz = (1 - j % 2) * (NZ // 2 + j // 2) + j % 2 * (NZ // 2 - (j + 1) // 2)
        return (z + dz) % NZ * NX + (x + dx) % NX

    def finish(source, target, sem):
        most = pl.ds(0, COUNT - 1)
        block((me + 1) % COUNT, source, most, target, most, sem).wait()

    def slot(t):
        return t % NX * NZ + t // NX

    def hop(half, dz, dx, to_z, to_x, recv_sem):
        owner = (half, (x + dx) % NX, (z + dz) % NZ)
        return pltpu.make_async_remote_copy(
            src_ref=uall.at[owner],
            dst_ref=uall.at[owner],
            send_sem=hop_send,
            recv_sem=recv_sem,
            device_id=(group, (z + to_z) % NZ * NX + (x + to_x) % NX),
            device_id_type=MESH,
        )

    def both_arrived(recv_sem):
        pltpu.make_async_copy(uall.at[:, 0, 0], uall.at[:, 0, 0], recv_sem).wait()

    def sideways(dz):
        for half in range(2):
            hop(half, dz, 0, 0, 1, side_recv.at[0, dz]).start()
            hop(half, dz, 0, 0, NX - 1, side_recv.at[1, dz]).start()

    def send_hidden(part_index):
        first, second = PARTS_0, PARTS_1
        start = first[part_index] + c * (second[part_index] - first[part_index])
        stop = first[part_index + 1] + c * (second[part_index + 1] - first[part_index + 1])

        @pl.loop(start, stop)
        def _(k):
            other = partner(k)
            block(other, hs, other, hr, me, h_sem).start()

    def forward(dz):
        both_arrived(side_recv.at[0, dz])
        hop(0, dz, NX - 1, 0, 1, pass_recv).start()
        both_arrived(side_recv.at[1, dz])
        hop(1, dz, 1, 0, NX - 1, pass_recv).start()

    with jax.named_scope("ring_along_z"):
        loads[1].wait()
        loads[2].wait()
        for half in range(2):
            hop(half, 0, 0, 1, 0, ring_recv.at[0, 0, half]).start()
            hop(half, 0, 0, NZ - 1, 0, ring_recv.at[1, 0, half]).start()
        sideways(0)
        loads[0].wait()
        send_hidden(0)
        for step in range(1, 4):
            for half in range(2):
                here = hop(half, NZ - step, 0, 1, 0, ring_recv.at[0, step - 1, half])
                here.wait_recv()
                if step < 3 or half == 0:
                    hop(half, NZ - step, 0, 1, 0, ring_recv.at[0, step, half]).start()
                here = hop(half, step, 0, NZ - 1, 0, ring_recv.at[1, step - 1, half])
                here.wait_recv()
                if step < 3 or half == 1:
                    hop(half, step, 0, NZ - 1, 0, ring_recv.at[1, step, half]).start()
            sideways(step)
            sideways(NZ - step)
            send_hidden(step)
            for dz in FORWARDS[step - 1]:
                forward(dz)
        hop(0, 4, 0, 1, 0, ring_recv.at[0, 3, 0]).wait_recv()
        hop(1, 4, 0, NZ - 1, 0, ring_recv.at[1, 3, 1]).wait_recv()
        sideways(4)
        send_hidden(4)
        for dz in FORWARDS[3]:
            forward(dz)

    def grad_group(dx):
        column = (x + dx) % NX
        total = dot_t(uall[0, column].reshape(NZ * ROWS, HALF), wv[:, pl.ds(0, HALF)])
        total += dot_t(uall[1, column].reshape(NZ * ROWS, HALF), wv[:, pl.ds(HALF, HALF)])
        gs[pl.ds(column * NZ, NZ)] = total.astype(BF16).reshape(NZ, ROWS, WIDTH)

    def send_grad(dx):
        column = (x + dx) % NX

        @pl.loop(0 if dx else 1, NZ)
        def _(dz):
            row = (z + dz) % NZ
            block(row * NX + column, gs, column * NZ + row, gr, me, g_sem).start()

    def due(when, only=None):
        for dx in (0, 1, 3, 2) if only is None else (only,):
            cores = [core for core in range(2) if GRADS[core][dx] == when]
            if len(cores) == 2:
                send_grad(dx)
            elif cores:
                pl.when(c == cores[0])(functools.partial(send_grad, dx))

    with jax.named_scope("first_grad"):
        loads[5].wait()
        grad_group(0)
        own_grad = pltpu.make_async_copy(gs.at[slot(me)], gr.at[me], own_sem.at[2])
        own_grad.start()

    loads[3].wait()
    loads[4].wait()
    with jax.named_scope("wait_hidden"):
        finish(hs, hr, h_sem)

    due(0)
    with jax.named_scope("more_along_x"):
        for dz in FORWARDS[4]:
            forward(dz)

    with jax.named_scope("rotate_hidden"):
        @pl.loop(0, 2)
        def _(m):
            rows = hr[pl.ds(m * 16, 16)].reshape(256, WIDTH)
            local[pl.ds(pl.multiple_of(m * 256, 256), 256), :] = dot(rows, kt[...])

    member = (
        lax.broadcasted_iota(jnp.int32, (128, 128), 0) // 32
        == lax.broadcasted_iota(jnp.int32, (128, 128), 1) // 32
    )
    mean_table = jnp.where(member, 1.0 / 32.0, 0.0).astype(BF16)

    with jax.named_scope("clip"):
        @pl.loop(0, TILES)
        def _(j):
            lanes = pl.ds(pl.multiple_of(j * 128, 128), 128)
            rotated = butterfly(local[:, lanes].reshape(COUNT, ROWS, 128)).reshape(COUNT * ROWS, 128)
            rotated = rotated * SCALE
            square = rotated * rotated
            high = square.astype(BF16)
            low = (square - high.astype(F32)).astype(BF16)
            mean_sq = dot(high, mean_table) + dot(low, mean_table)
            floored = jnp.maximum(mean_sq, MEAN_FLOOR)
            inverse = lax.rsqrt(floored)
            squash = jnp.tanh(rotated * (0.5 * inverse))
            clipped = (2.0 * floored * inverse * squash).astype(BF16)
            cs[:, :, lanes] = clipped.reshape(COUNT, ROWS, 128)
            gate[:, :, lanes] = (1.0 - squash * squash).reshape(COUNT, ROWS, 128)

    with jax.named_scope("send_clipped"):
        @pl.loop(0, COUNT - 1)
        def _(k):
            other = partner(k)
            block(other, cs, other, cr, slot(me), c_sem).start()

        own_clipped = pltpu.make_async_copy(cs.at[me], cr.at[slot(me)], own_sem.at[1])
        own_clipped.start()

    with jax.named_scope("rest_along_x"):
        for dz in FORWARDS[5]:
            forward(dz)
    with jax.named_scope("near_grad"):
        due(1, 0)
        for dx in (1, NX - 1):
            grad_group(dx)
            due(1, dx)
    with jax.named_scope("wait_gather"):
        pltpu.make_async_copy(uall.at[:, 0], uall.at[:, 0], pass_recv).wait()
    def last_grad():
        with jax.named_scope("last_grad"):
            grad_group(2)
            due(1, 2)

    if not LAST_AFTER:
        last_grad()

    own_clipped.wait()
    with jax.named_scope("wait_clipped"):
        finish(cs, cr, c_sem)
    due(2)

    @pl.loop(0, TILES)
    def _(j):
        lanes = pl.ds(pl.multiple_of(j * 128, 128), 128)
        ct[lanes, :] = cr[:, :, lanes].reshape(COUNT * ROWS, 128).T

    def columns(n):
        return pl.ds(pl.multiple_of(n * STRIP, STRIP), STRIP)

    def rows_of(owner):
        return pl.ds(pl.multiple_of(owner * PIECE, 16), PIECE)

    def to_core(n, q):
        return pltpu.make_async_remote_copy(
            src_ref=part.at[rows_of(2 * q + 1 - c), columns(n)],
            dst_ref=core_in.at[q, :, columns(n)],
            send_sem=core_send,
            recv_sem=core_recv.at[n],
            device_id=(2 * y + 1 - c, me),
            device_id_type=MESH,
        )

    def to_y(n, owner, target, landing, recv_sem):
        return pltpu.make_async_remote_copy(
            src_ref=ysend.at[owner, :, columns(n)],
            dst_ref=landing,
            send_sem=y_send,
            recv_sem=recv_sem,
            device_id=(2 * target + c, me),
            device_id_type=MESH,
        )

    def far(n):
        way = 1 + 2 * (n // HALF_STRIPS)
        return to_y(n, (y + 2) % 4, (y + way) % 4, passing.at[:, columns(n)], far_recv.at[n])

    def direct(n):
        back = (y + 3 - 2 * (n // HALF_STRIPS)) % 4
        return to_y(n, back, back, yin.at[0, :, columns(n)], y_recv)

    def joined(n):
        ahead = (y + 1 + 2 * (n // HALF_STRIPS)) % 4
        return to_y(n, ahead, ahead, yin.at[1, :, columns(n)], y_recv)

    def pair(n, q):
        both = part[rows_of(2 * q + c), columns(n)].astype(F32)
        return both + core_in[q, :, columns(n)].astype(F32)

    def send_far(n):
        pltpu.make_async_copy(core_in.at[:, :, columns(n)], core_in.at[:, :, columns(n)], core_recv.at[n]).wait()
        q = (y + 2) % 4
        ysend[q, :, columns(n)] = pair(n, q).astype(BF16)
        far(n).start()

    def send_direct(n):
        q = (y + 3 - 2 * (n // HALF_STRIPS)) % 4
        ysend[q, :, columns(n)] = pair(n, q).astype(BF16)
        direct(n).start()

    def join(n):
        q = (y + 1 + 2 * (n // HALF_STRIPS)) % 4
        far(n).wait_recv()
        both = pair(n, q) + passing[:, columns(n)].astype(F32)
        ysend[q, :, columns(n)] = both.astype(BF16)
        joined(n).start()

    def turn(i):
        return (i % 2) * HALF_STRIPS + i // 2

    with jax.named_scope("weight_term"):
        @pl.loop(0, STRIPS)
        def _(i):
            n = turn(i)
            start = pl.multiple_of(n % HALF_STRIPS * STRIP, STRIP)
            tokens = uall[n // HALF_STRIPS, :, :, :, pl.ds(start, STRIP)].reshape(COUNT * ROWS, STRIP)
            term = dot(ct[...], tokens) * (1.0 / 64.0)
            part[:, columns(n)] = term.astype(BF16)

            @pl.loop(0, 4)
            def _(k):
                to_core(n, (y + 2 + k) % 4).start()

            @pl.when((i > 0) & (c == 0))
            def _():
                send_far(turn(i - 1))

        if LAST_AFTER:
            last_grad()
        due(3)

    with jax.named_scope("far_along_y"):
        @pl.loop((1 - c) * (STRIPS - 1), STRIPS)
        def _(i):
            send_far(turn(i))

    due(4)

    with jax.named_scope("direct_along_y"):
        @pl.loop(0, STRIPS)
        def _(i):
            send_direct(turn(i))

    own_grad.wait()
    with jax.named_scope("wait_grad"):
        finish(gs, gr, g_sem)

    with jax.named_scope("rotate_grad"):
        @pl.loop(0, TILES)
        def _(j):
            lanes = pl.ds(pl.multiple_of(j * 128, 128), 128)
            gated = gate[:, :, lanes] * gr[:, :, lanes].astype(F32)
            ps[:, lanes] = butterfly(gated).reshape(COUNT * ROWS, 128).astype(BF16)

        @pl.loop(0, 2)
        def _(m):
            rows = ps[pl.ds(pl.multiple_of(m * 256, 256), 256), :]
            rs[pl.ds(m * 16, 16)] = (dot(rows, kt[...]) * SCALE).astype(BF16).reshape(16, ROWS, WIDTH)

            @pl.loop(m * 16, m * 16 + 16)
            def _(i):
                @pl.when(i != me)
                def _():
                    block(i, rs, i, out_ref, me, r_sem).start()

        own_result = pltpu.make_async_copy(rs.at[me], out_ref.at[me], own_sem.at[3])
        own_result.start()

    with jax.named_scope("join_along_y"):
        @pl.loop(0, STRIPS)
        def _(i):
            join(turn(i))

    with jax.named_scope("wait_along_y"):
        pltpu.make_async_copy(yin, yin, y_recv).wait()

    with jax.named_scope("last_sum"):
        @pl.loop(0, STRIPS)
        def _(n):
            both = pair(n, y)
            for lane in range(2):
                both += yin[lane, :, columns(n)].astype(F32)
            wout[:, columns(n)] = both.astype(BF16)

    out_copy = pltpu.make_async_copy(wout, wout_ref, own_sem.at[4])
    out_copy.start()

    pltpu.make_async_copy(core_in, core_in, core_send).wait()
    pltpu.make_async_copy(ysend.at[pl.ds(0, 3)], ysend.at[pl.ds(0, 3)], y_send).wait()
    sent = uall.at[:, :, pl.ds(0, NZ - 1)]
    pltpu.make_async_copy(sent, sent, hop_send).wait()
    sent = uall.at[:, pl.ds(0, 3), 0]
    pltpu.make_async_copy(sent, sent, hop_send).wait()
    own_result.wait()
    with jax.named_scope("wait_result"):
        finish(rs, out_ref, r_sem)
    out_copy.wait()


def settle(input_grad, weight_grad, input_out, weight_out, input_held, weight_held, sem):
    def steps(source, held, target, lane):
        cuts = [pl.ds(0, 16), pl.ds(16, source.shape[0] - 16)]
        first = [pltpu.make_async_copy(source.at[c], held.at[c], sem.at[lane, i]) for i, c in enumerate(cuts)]
        second = [pltpu.make_async_copy(held.at[c], target.at[c], sem.at[lane, i + 2]) for i, c in enumerate(cuts)]
        return list(zip(first, second))

    every = steps(input_grad, input_held, input_out, 0) + steps(weight_grad, weight_held, weight_out, 1)
    for first, second in every:
        first.start()
    for first, second in every:
        first.wait()
        second.start()
    for first, second in every:
        second.wait()


def on_device(hidden_act, upstream, rotated_weight):
    table = jnp.asarray(np.kron(walsh_table(32), paley_table()), BF16)
    blocks = (COUNT, ROWS, WIDTH)
    sems = pltpu.SemaphoreType.DMA
    input_grad, weight_grad = pl.pallas_call(
        kernel,
        out_shape=(
            jax.ShapeDtypeStruct(blocks, BF16),
            jax.ShapeDtypeStruct((PIECE, D), BF16),
        ),
        in_specs=[pl.BlockSpec(memory_space=pl.ANY)] * 4,
        out_specs=[pl.BlockSpec(memory_space=pl.ANY)] * 2,
        scratch_shapes=[
            pltpu.VMEM(blocks, BF16),
            pltpu.VMEM(blocks, BF16),
            pltpu.VMEM((WIDTH, WIDTH), BF16),
            pltpu.VMEM((2, NX, NZ, ROWS, HALF), BF16),
            pltpu.VMEM((WIDTH, D), BF16),
            pltpu.VMEM((COUNT * ROWS, WIDTH), F32),
            pltpu.VMEM(blocks, F32),
            pltpu.VMEM(blocks, BF16),
            pltpu.VMEM(blocks, BF16),
            pltpu.VMEM((WIDTH, COUNT * ROWS), BF16),
            pltpu.VMEM(blocks, BF16),
            pltpu.VMEM(blocks, BF16),
            pltpu.VMEM((COUNT * ROWS, WIDTH), BF16),
            pltpu.VMEM(blocks, BF16),
            pltpu.VMEM((WIDTH, D), BF16),
            pltpu.VMEM((4, PIECE, D), BF16),
            pltpu.VMEM((4, PIECE, D), BF16),
            pltpu.VMEM((2, PIECE, D), BF16),
            pltpu.VMEM((PIECE, D), BF16),
            pltpu.VMEM((PIECE, D), BF16),
            sems((5,)),
            sems((5,)),
            sems((2,)), sems((2,)), sems((2,)), sems((2,)),
            sems, sems((2, 4, 2)), sems((2, NZ)), sems,
            sems, sems((STRIPS,)), sems, sems((STRIPS,)), sems,
        ],
        compiler_params=pltpu.CompilerParams(
            collective_id=0, has_side_effects=True, vmem_limit_bytes=60 << 20
        ),
    )(hidden_act.reshape(blocks), upstream, table, rotated_weight)
    input_grad, weight_grad = pl.pallas_call(
        settle,
        out_shape=(
            jax.ShapeDtypeStruct(blocks, BF16),
            jax.ShapeDtypeStruct((PIECE, D), BF16),
        ),
        in_specs=[pl.BlockSpec(memory_space=pl.ANY)] * 2,
        out_specs=[pl.BlockSpec(memory_space=pl.ANY)] * 2,
        scratch_shapes=[pltpu.VMEM(blocks, BF16), pltpu.VMEM((PIECE, D), BF16), sems((2, 4))],
    )(input_grad, weight_grad)
    return input_grad.reshape(COUNT * ROWS, WIDTH), weight_grad


def solution(mesh):
    placed = (P("dp", "tensor"), P(("dp", "tensor"), None), P("tensor", None))
    return jax.shard_map(
        on_device,
        mesh=mesh,
        in_specs=placed,
        out_specs=(P("dp", "tensor"), P(("tensor", "dp"), None)),
        check_vma=False,
    )
```

```python
import functools
import math

import jax
import jax.numpy as jnp
import numpy as np
from jax import lax
from jax.experimental import pallas as pl
from jax.experimental.pallas import tpu as pltpu
from jax.sharding import PartitionSpec as P

FF = 28672
MEAN_FLOOR = 0.04
MESH = pl.DeviceIdType.MESH


def paley_table():
    modulus = 13
    residues = set((value_index * value_index % modulus for value_index in range(1, modulus)))
    conference = np.zeros((modulus + 1, modulus + 1))
    conference[0, 1:] = 1.0
    conference[1:, 0] = 1.0
    for row_index in range(modulus):
        for column_index in range(modulus):
            if row_index != column_index:
                conference[1 + row_index, 1 + column_index] = (
                    1.0 if (column_index - row_index) % modulus in residues else -1.0
                )
    plus_block = np.array([[1.0, 1.0], [1.0, -1.0]])
    minus_block = np.array([[1.0, -1.0], [-1.0, -1.0]])
    return np.kron(conference, plus_block) + np.kron(np.eye(modulus + 1), minus_block)


def walsh_table(length):
    index = np.arange(length)
    both = index[:, None] & index[None, :]
    parity = np.zeros((length, length), np.int64)
    for bit in range(length.bit_length()):
        parity += both >> bit & 1
    return 1.0 - 2.0 * (parity % 2)


NZ, NX = 8, 4
COUNT = NZ * NX
ROWS = 16
WIDTH = 896
D = 4096
HALF = D // 2
PIECE = 112
STRIP = 512
STRIPS = D // STRIP
HALF_STRIPS = STRIPS // 2
SCALE = 1.0 / math.sqrt(FF)
TILES = WIDTH // 128
PARTS_0 = (0, 0, 0, 8, 31, 31)
PARTS_1 = (0, 0, 8, 20, 31, 31)
FORWARDS = ((), (), (), (0, 1, 7, 2, 6), (), (3, 5, 4))
LAST_AFTER = False
GRADS = ((1, 1, 1, 1), (1, 3, 3, 3))
F32 = jnp.float32
BF16 = jnp.bfloat16


def butterfly(values):
    shape = values.shape
    for bit in range(5):
        pairs = values.reshape(COUNT >> bit + 1, 2, 1 << bit, shape[1], shape[2])
        low, high = pairs[:, 0], pairs[:, 1]
        values = jnp.stack([low + high, low - high], axis=1).reshape(shape)
    return values


def dot(left, right):
    return lax.dot_general(left, right, (((1,), (0,)), ((), ())), preferred_element_type=F32)


def dot_t(left, right):
    return lax.dot_general(left, right, (((1,), (1,)), ((), ())), preferred_element_type=F32)


def kernel(
    hidden, upstream, table, weight, out_ref, wout_ref,
    hs, hr, kt, uall, wv, local, gate, cs, cr, ct, gs, gr, ps, rs, part, core_in, ysend, yin, passing, wout,
    local_sem, own_sem, h_sem, c_sem, g_sem, r_sem, hop_send, ring_recv, side_recv, pass_recv,
    core_send, core_recv, y_send, far_recv, y_recv,
):
    group = lax.axis_index("dp")
    me = lax.axis_index("tensor")
    z, x = me // NX, me % NX
    y, c = group // 2, group % 2

    loads = [
        pltpu.make_async_copy(hidden, hs, local_sem.at[0]),
        pltpu.make_async_copy(upstream.at[:, pl.ds(0, HALF)], uall.at[0, x, z], local_sem.at[1]),
        pltpu.make_async_copy(upstream.at[:, pl.ds(HALF, HALF)], uall.at[1, x, z], local_sem.at[2]),
        pltpu.make_async_copy(hidden.at[me], hr.at[me], own_sem.at[0]),
        pltpu.make_async_copy(table, kt, local_sem.at[3]),
        pltpu.make_async_copy(weight, wv, local_sem.at[4]),
    ]
    for load in loads:
        load.start()

    barrier = pltpu.get_barrier_semaphore()

    def greet(device):
        pl.semaphore_signal(barrier, inc=1, device_id=device, device_id_type=MESH)

    @pl.loop(1, COUNT)
    def _(k):
        greet((group, (me + k) % COUNT))

    greet((2 * y + 1 - c, me))

    @pl.loop(1, 4)
    def _(k):
        greet((2 * ((y + k) % 4) + c, me))

    with jax.named_scope("entry"):
        pl.semaphore_wait(barrier, COUNT - 1 + 1 + 3)

    def block(other, source, place_here, target, place_there, sem):
        return pltpu.make_async_remote_copy(
            src_ref=source.at[place_here],
            dst_ref=target.at[place_there],
            send_sem=sem.at[0],
            recv_sem=sem.at[1],
            device_id=(group, other),
            device_id_type=MESH,
        )

    def partner(k):
        j, dx = k // NX, (k + 1) % NX
        dz = (1 - j % 2) * (NZ // 2 + j // 2) + j % 2 * (NZ // 2 - (j + 1) // 2)
        return (z + dz) % NZ * NX + (x + dx) % NX

    def finish(source, target, sem):
        most = pl.ds(0, COUNT - 1)
        block((me + 1) % COUNT, source, most, target, most, sem).wait()

    def slot(t):
        return t % NX * NZ + t // NX

    def hop(half, dz, dx, to_z, to_x, recv_sem):
        owner = (half, (x + dx) % NX, (z + dz) % NZ)
        return pltpu.make_async_remote_copy(
            src_ref=uall.at[owner],
            dst_ref=uall.at[owner],
            send_sem=hop_send,
            recv_sem=recv_sem,
            device_id=(group, (z + to_z) % NZ * NX + (x + to_x) % NX),
            device_id_type=MESH,
        )

    def both_arrived(recv_sem):
        pltpu.make_async_copy(uall.at[:, 0, 0], uall.at[:, 0, 0], recv_sem).wait()

    def sideways(dz):
        for half in range(2):
            hop(half, dz, 0, 0, 1, side_recv.at[0, dz]).start()
            hop(half, dz, 0, 0, NX - 1, side_recv.at[1, dz]).start()

    def send_hidden(part_index):
        first, second = PARTS_0, PARTS_1
        start = first[part_index] + c * (second[part_index] - first[part_index])
        stop = first[part_index + 1] + c * (second[part_index + 1] - first[part_index + 1])

        @pl.loop(start, stop)
        def _(k):
            other = partner(k)
            block(other, hs, other, hr, me, h_sem).start()

    def forward(dz):
        both_arrived(side_recv.at[0, dz])
        hop(0, dz, NX - 1, 0, 1, pass_recv).start()
        both_arrived(side_recv.at[1, dz])
        hop(1, dz, 1, 0, NX - 1, pass_recv).start()

    with jax.named_scope("ring_along_z"):
        loads[1].wait()
        loads[2].wait()
        for half in range(2):
            hop(half, 0, 0, 1, 0, ring_recv.at[0, 0, half]).start()
            hop(half, 0, 0, NZ - 1, 0, ring_recv.at[1, 0, half]).start()
        sideways(0)
        loads[0].wait()
        send_hidden(0)
        for step in range(1, 4):
            for half in range(2):
                here = hop(half, NZ - step, 0, 1, 0, ring_recv.at[0, step - 1, half])
                here.wait_recv()
                if step < 3 or half == 0:
                    hop(half, NZ - step, 0, 1, 0, ring_recv.at[0, step, half]).start()
                here = hop(half, step, 0, NZ - 1, 0, ring_recv.at[1, step - 1, half])
                here.wait_recv()
                if step < 3 or half == 1:
                    hop(half, step, 0, NZ - 1, 0, ring_recv.at[1, step, half]).start()
            sideways(step)
            sideways(NZ - step)
            send_hidden(step)
            for dz in FORWARDS[step - 1]:
                forward(dz)
        hop(0, 4, 0, 1, 0, ring_recv.at[0, 3, 0]).wait_recv()
        hop(1, 4, 0, NZ - 1, 0, ring_recv.at[1, 3, 1]).wait_recv()
        sideways(4)
        send_hidden(4)
        for dz in FORWARDS[3]:
            forward(dz)

    def grad_group(dx):
        column = (x + dx) % NX
        total = dot_t(uall[0, column].reshape(NZ * ROWS, HALF), wv[:, pl.ds(0, HALF)])
        total += dot_t(uall[1, column].reshape(NZ * ROWS, HALF), wv[:, pl.ds(HALF, HALF)])
        gs[pl.ds(column * NZ, NZ)] = total.astype(BF16).reshape(NZ, ROWS, WIDTH)

    def send_grad(dx):
        column = (x + dx) % NX

        @pl.loop(0 if dx else 1, NZ)
        def _(dz):
            row = (z + dz) % NZ
            block(row * NX + column, gs, column * NZ + row, gr, me, g_sem).start()

    def due(when, only=None):
        for dx in (0, 1, 3, 2) if only is None else (only,):
            cores = [core for core in range(2) if GRADS[core][dx] == when]
            if len(cores) == 2:
                send_grad(dx)
            elif cores:
                pl.when(c == cores[0])(functools.partial(send_grad, dx))

    with jax.named_scope("first_grad"):
        loads[5].wait()
        grad_group(0)
        own_grad = pltpu.make_async_copy(gs.at[slot(me)], gr.at[me], own_sem.at[2])
        own_grad.start()

    loads[3].wait()
    loads[4].wait()
    with jax.named_scope("wait_hidden"):
        finish(hs, hr, h_sem)

    due(0)
    with jax.named_scope("more_along_x"):
        for dz in FORWARDS[4]:
            forward(dz)

    with jax.named_scope("rotate_hidden"):
        @pl.loop(0, 2)
        def _(m):
            rows = hr[pl.ds(m * 16, 16)].reshape(256, WIDTH)
            local[pl.ds(pl.multiple_of(m * 256, 256), 256), :] = dot(rows, kt[...])

    member = (
        lax.broadcasted_iota(jnp.int32, (128, 128), 0) // 32
        == lax.broadcasted_iota(jnp.int32, (128, 128), 1) // 32
    )
    mean_table = jnp.where(member, 1.0 / 32.0, 0.0).astype(BF16)

    with jax.named_scope("clip"):
        def clip(j):
            lanes = pl.ds(pl.multiple_of(j * 128, 128), 128)
            rotated = butterfly(local[:, lanes].reshape(COUNT, ROWS, 128)).reshape(COUNT * ROWS, 128)
            rotated = rotated * SCALE
            square = rotated * rotated
            high = square.astype(BF16)
            low = (square - high.astype(F32)).astype(BF16)
            mean_sq = dot(high, mean_table) + dot(low, mean_table)
            floored = jnp.maximum(mean_sq, MEAN_FLOOR)
            inverse = lax.rsqrt(floored)
            squash = jnp.tanh(rotated * (0.5 * inverse))
            clipped = (2.0 * floored * inverse * squash).astype(BF16)
            cs[:, :, lanes] = clipped.reshape(COUNT, ROWS, 128)
            gate[:, :, lanes] = (1.0 - squash * squash).reshape(COUNT, ROWS, 128)

    with jax.named_scope("send_clipped"):
        for first, last in ((0, 4), (4, TILES)):
            pl.loop(first, last)(clip)
            piece = (slice(None), pl.ds(first * 128, (last - first) * 128))

            @pl.loop(0, COUNT - 1)
            def _(k):
                other = partner(k)
                block(other, cs, (other, *piece), cr, (slot(me), *piece), c_sem).start()

        own_clipped = pltpu.make_async_copy(cs.at[me], cr.at[slot(me)], own_sem.at[1])
        own_clipped.start()

    with jax.named_scope("rest_along_x"):
        for dz in FORWARDS[5]:
            forward(dz)
    with jax.named_scope("near_grad"):
        due(1, 0)
        for dx in (1, NX - 1):
            grad_group(dx)
            due(1, dx)
    with jax.named_scope("wait_gather"):
        pltpu.make_async_copy(uall.at[:, 0], uall.at[:, 0], pass_recv).wait()
    def last_grad():
        with jax.named_scope("last_grad"):
            grad_group(2)
            due(1, 2)

    if not LAST_AFTER:
        last_grad()

    own_clipped.wait()
    with jax.named_scope("wait_clipped"):
        finish(cs, cr, c_sem)
    due(2)

    @pl.loop(0, TILES)
    def _(j):
        lanes = pl.ds(pl.multiple_of(j * 128, 128), 128)
        ct[lanes, :] = cr[:, :, lanes].reshape(COUNT * ROWS, 128).T

    def columns(n):
        return pl.ds(pl.multiple_of(n * STRIP, STRIP), STRIP)

    def rows_of(owner):
        return pl.ds(pl.multiple_of(owner * PIECE, 16), PIECE)

    def to_core(n, q):
        return pltpu.make_async_remote_copy(
            src_ref=part.at[rows_of(2 * q + 1 - c), columns(n)],
            dst_ref=core_in.at[q, :, columns(n)],
            send_sem=core_send,
            recv_sem=core_recv.at[n],
            device_id=(2 * y + 1 - c, me),
            device_id_type=MESH,
        )

    def to_y(n, owner, target, landing, recv_sem):
        return pltpu.make_async_remote_copy(
            src_ref=ysend.at[owner, :, columns(n)],
            dst_ref=landing,
            send_sem=y_send,
            recv_sem=recv_sem,
            device_id=(2 * target + c, me),
            device_id_type=MESH,
        )

    def far(n):
        way = 1 + 2 * (n // HALF_STRIPS)
        return to_y(n, (y + 2) % 4, (y + way) % 4, passing.at[:, columns(n)], far_recv.at[n])

    def direct(n):
        back = (y + 3 - 2 * (n // HALF_STRIPS)) % 4
        return to_y(n, back, back, yin.at[0, :, columns(n)], y_recv)

    def joined(n):
        ahead = (y + 1 + 2 * (n // HALF_STRIPS)) % 4
        return to_y(n, ahead, ahead, yin.at[1, :, columns(n)], y_recv)

    def pair(n, q):
        both = part[rows_of(2 * q + c), columns(n)].astype(F32)
        return both + core_in[q, :, columns(n)].astype(F32)

    def send_far(n):
        pltpu.make_async_copy(core_in.at[:, :, columns(n)], core_in.at[:, :, columns(n)], core_recv.at[n]).wait()
        q = (y + 2) % 4
        ysend[q, :, columns(n)] = pair(n, q).astype(BF16)
        far(n).start()

    def send_direct(n):
        q = (y + 3 - 2 * (n // HALF_STRIPS)) % 4
        ysend[q, :, columns(n)] = pair(n, q).astype(BF16)
        direct(n).start()

    def join(n):
        q = (y + 1 + 2 * (n // HALF_STRIPS)) % 4
        far(n).wait_recv()
        both = pair(n, q) + passing[:, columns(n)].astype(F32)
        ysend[q, :, columns(n)] = both.astype(BF16)
        joined(n).start()

    def turn(i):
        return (i % 2) * HALF_STRIPS + i // 2

    with jax.named_scope("weight_term"):
        @pl.loop(0, STRIPS)
        def _(i):
            n = turn(i)
            start = pl.multiple_of(n % HALF_STRIPS * STRIP, STRIP)
            tokens = uall[n // HALF_STRIPS, :, :, :, pl.ds(start, STRIP)].reshape(COUNT * ROWS, STRIP)
            term = dot(ct[...], tokens) * (1.0 / 64.0)
            part[:, columns(n)] = term.astype(BF16)

            @pl.loop(0, 4)
            def _(k):
                to_core(n, (y + 2 + k) % 4).start()

            @pl.when((i > 0) & (c == 0))
            def _():
                send_far(turn(i - 1))

        if LAST_AFTER:
            last_grad()
        due(3)

    with jax.named_scope("far_along_y"):
        @pl.loop((1 - c) * (STRIPS - 1), STRIPS)
        def _(i):
            send_far(turn(i))

    due(4)

    with jax.named_scope("direct_along_y"):
        @pl.loop(0, STRIPS)
        def _(i):
            send_direct(turn(i))

    own_grad.wait()
    with jax.named_scope("wait_grad"):
        finish(gs, gr, g_sem)

    with jax.named_scope("rotate_grad"):
        @pl.loop(0, TILES)
        def _(j):
            lanes = pl.ds(pl.multiple_of(j * 128, 128), 128)
            gated = gate[:, :, lanes] * gr[:, :, lanes].astype(F32)
            ps[:, lanes] = butterfly(gated).reshape(COUNT * ROWS, 128).astype(BF16)

        @pl.loop(0, 2)
        def _(m):
            rows = ps[pl.ds(pl.multiple_of(m * 256, 256), 256), :]
            rs[pl.ds(m * 16, 16)] = (dot(rows, kt[...]) * SCALE).astype(BF16).reshape(16, ROWS, WIDTH)

            @pl.loop(m * 16, m * 16 + 16)
            def _(i):
                @pl.when(i != me)
                def _():
                    block(i, rs, i, out_ref, me, r_sem).start()

        own_result = pltpu.make_async_copy(rs.at[me], out_ref.at[me], own_sem.at[3])
        own_result.start()

    with jax.named_scope("join_along_y"):
        @pl.loop(0, STRIPS)
        def _(i):
            join(turn(i))

    with jax.named_scope("wait_along_y"):
        pltpu.make_async_copy(yin, yin, y_recv).wait()

    with jax.named_scope("last_sum"):
        @pl.loop(0, STRIPS)
        def _(n):
            both = pair(n, y)
            for lane in range(2):
                both += yin[lane, :, columns(n)].astype(F32)
            wout[:, columns(n)] = both.astype(BF16)

    out_copy = pltpu.make_async_copy(wout, wout_ref, own_sem.at[4])
    out_copy.start()

    pltpu.make_async_copy(core_in, core_in, core_send).wait()
    pltpu.make_async_copy(ysend.at[pl.ds(0, 3)], ysend.at[pl.ds(0, 3)], y_send).wait()
    sent = uall.at[:, :, pl.ds(0, NZ - 1)]
    pltpu.make_async_copy(sent, sent, hop_send).wait()
    sent = uall.at[:, pl.ds(0, 3), 0]
    pltpu.make_async_copy(sent, sent, hop_send).wait()
    own_result.wait()
    with jax.named_scope("wait_result"):
        finish(rs, out_ref, r_sem)
    out_copy.wait()


def settle(input_grad, weight_grad, input_out, weight_out, input_held, weight_held, sem):
    def steps(source, held, target, lane):
        cuts = [pl.ds(0, 16), pl.ds(16, source.shape[0] - 16)]
        first = [pltpu.make_async_copy(source.at[c], held.at[c], sem.at[lane, i]) for i, c in enumerate(cuts)]
        second = [pltpu.make_async_copy(held.at[c], target.at[c], sem.at[lane, i + 2]) for i, c in enumerate(cuts)]
        return list(zip(first, second))

    every = steps(input_grad, input_held, input_out, 0) + steps(weight_grad, weight_held, weight_out, 1)
    for first, second in every:
        first.start()
    for first, second in every:
        first.wait()
        second.start()
    for first, second in every:
        second.wait()


def on_device(hidden_act, upstream, rotated_weight):
    table = jnp.asarray(np.kron(walsh_table(32), paley_table()), BF16)
    blocks = (COUNT, ROWS, WIDTH)
    sems = pltpu.SemaphoreType.DMA
    input_grad, weight_grad = pl.pallas_call(
        kernel,
        out_shape=(
            jax.ShapeDtypeStruct(blocks, BF16),
            jax.ShapeDtypeStruct((PIECE, D), BF16),
        ),
        in_specs=[pl.BlockSpec(memory_space=pl.ANY)] * 4,
        out_specs=[pl.BlockSpec(memory_space=pl.ANY)] * 2,
        scratch_shapes=[
            pltpu.VMEM(blocks, BF16),
            pltpu.VMEM(blocks, BF16),
            pltpu.VMEM((WIDTH, WIDTH), BF16),
            pltpu.VMEM((2, NX, NZ, ROWS, HALF), BF16),
            pltpu.VMEM((WIDTH, D), BF16),
            pltpu.VMEM((COUNT * ROWS, WIDTH), F32),
            pltpu.VMEM(blocks, F32),
            pltpu.VMEM(blocks, BF16),
            pltpu.VMEM(blocks, BF16),
            pltpu.VMEM((WIDTH, COUNT * ROWS), BF16),
            pltpu.VMEM(blocks, BF16),
            pltpu.VMEM(blocks, BF16),
            pltpu.VMEM((COUNT * ROWS, WIDTH), BF16),
            pltpu.VMEM(blocks, BF16),
            pltpu.VMEM((WIDTH, D), BF16),
            pltpu.VMEM((4, PIECE, D), BF16),
            pltpu.VMEM((4, PIECE, D), BF16),
            pltpu.VMEM((2, PIECE, D), BF16),
            pltpu.VMEM((PIECE, D), BF16),
            pltpu.VMEM((PIECE, D), BF16),
            sems((5,)),
            sems((5,)),
            sems((2,)), sems((2,)), sems((2,)), sems((2,)),
            sems, sems((2, 4, 2)), sems((2, NZ)), sems,
            sems, sems((STRIPS,)), sems, sems((STRIPS,)), sems,
        ],
        compiler_params=pltpu.CompilerParams(
            collective_id=0, has_side_effects=True, vmem_limit_bytes=60 << 20
        ),
    )(hidden_act.reshape(blocks), upstream, table, rotated_weight)
    input_grad, weight_grad = pl.pallas_call(
        settle,
        out_shape=(
            jax.ShapeDtypeStruct(blocks, BF16),
            jax.ShapeDtypeStruct((PIECE, D), BF16),
        ),
        in_specs=[pl.BlockSpec(memory_space=pl.ANY)] * 2,
        out_specs=[pl.BlockSpec(memory_space=pl.ANY)] * 2,
        scratch_shapes=[pltpu.VMEM(blocks, BF16), pltpu.VMEM((PIECE, D), BF16), sems((2, 4))],
    )(input_grad, weight_grad)
    return input_grad.reshape(COUNT * ROWS, WIDTH), weight_grad


def solution(mesh):
    placed = (P("dp", "tensor"), P(("dp", "tensor"), None), P("tensor", None))
    return jax.shard_map(
        on_device,
        mesh=mesh,
        in_specs=placed,
        out_specs=(P("dp", "tensor"), P(("tensor", "dp"), None)),
        check_vma=False,
    )
```
